32 devices in a mesh: freq: 8 (over y, x, core), src: 4 (over z).
Axes of the slice: x: 2, y: 2, z: 4, core: 2. Of those that a mesh axis runs over, the one named last changes fastest.
Arguments:
- focusing: bfloat16 [32, 1024, 2048], P('src', 'freq'), may hold values from -6 to 6
- direct: bfloat16 [32, 1024, 2048], P('src', 'freq'), may hold values from -6 to 6
- kernel: bfloat16 [2, 192, 2048, 1024], P(None, 'freq', 'src'), may hold values from -0.125 to 0.125
- onset_up: int32 [32, 2048], P('freq', 'src'), may hold values from 256 to 2048
- onset_back: int32 [32, 1024], P('src', 'freq'), may hold values from 256 to 2048
Outputs:
- upgoing: bfloat16 [32, 2048, 2048], P('freq', 'src')
- updated: bfloat16 [32, 1024, 2048], P('src', 'freq')
The draws below stay inside these ranges and needn't reach their ends.
All inputs are finite; a program needn't handle non-finite values.
Results may differ from the reference program's by a relative error of at most 0.008.
Values may be sent and summed in bfloat16 or wider, within the bound.
A program may use at most 128 MiB of HBM per device.

```python
import math
import jax
import jax.numpy as jnp
from jax import lax

NT = 2048
NF = 192
BIN0 = 16
S = 2048
R = 1024
P_SIZE = 32
N_SRC = 4


def with_ends(result, rng, least, largest):
    dims = result.shape
    spot = [jax.random.randint(jax.random.fold_in(rng, axis), (), 0, dims[axis]) for axis in range(len(dims))]
    result = result.at[tuple(spot)].set(least)
    longest = dims.index(max(dims))
    spot[longest] = (spot[longest] + 1) % dims[longest]
    return result.at[tuple(spot)].set(largest)


def shard_levels(key, dims, split, least, top_value):
    gain, own = 1.0, jax.random.fold_in(key, 6)
    for dim, parts in split:
        steps = jnp.exp(jax.random.uniform(jax.random.fold_in(own, dim), (parts,), jnp.float32, least / len(split), top_value / len(split)))
        gain = gain * jnp.repeat(steps, dims[dim] // parts).reshape([-1 if axis == dim else 1 for axis in range(len(dims))])
    return gain


def gaussian(key, shape, width, limit, split=(), kind=jnp.bfloat16):
    entries = width * jax.random.normal(key, shape, jnp.float32)
    if split:
        entries = entries * shard_levels(key, shape, split, -0.22, 0.18)
    return jnp.clip(entries, -limit, limit).astype(kind)


def setup_inputs(seed: int = 0) -> dict:
    key_list = jax.random.split(jax.random.key(seed), 6)
    return {
        "focusing": gaussian(key_list[0], (P_SIZE, R, NT), 1.0, 6.0, ((0, 4), (1, 8))),
        "direct": gaussian(key_list[1], (P_SIZE, R, NT), 1.0, 6.0, ((0, 4), (1, 8))),
        "kernel": gaussian(key_list[2], (2, NF, S, R), (2 * R) ** -0.5, 0.125, ((1, 8), (2, 4))),
        "onset_up": with_ends(jax.random.randint(key_list[3], (P_SIZE, S), NT // 8, NT + 1), jax.random.fold_in(key_list[3], 1), NT // 8, NT).astype(jnp.int32),
        "onset_back": with_ends(jax.random.randint(key_list[4], (P_SIZE, R), NT // 8, NT + 1), jax.random.fold_in(key_list[4], 1), NT // 8, NT).astype(jnp.int32),
    }


def frequency_band_tables():
    sample_index = jnp.arange(NT, dtype=jnp.int32)
    bin_index = BIN0 + jnp.arange(NF, dtype=jnp.int32)
    phase = (sample_index[:, None] * bin_index[None, :]) % NT
    angle = phase.astype(jnp.float32) * (2.0 * math.pi / NT)
    cosine = jnp.cos(angle)
    sine = jnp.sin(angle)
    forward_table = jnp.stack([cosine, -sine], axis=2).reshape(NT, 2 * NF).astype(jnp.bfloat16)
    inverse_table = ((2.0 / NT) * jnp.stack([cosine.T, -sine.T], axis=1)).reshape(2 * NF, NT).astype(jnp.bfloat16)
    return forward_table, inverse_table


def reference(focusing, direct, kernel, onset_up, onset_back):
    forward_table, inverse_table = frequency_band_tables()
    highest = lax.Precision.HIGHEST
    spectrum = jnp.dot(focusing.reshape(P_SIZE * R, NT), forward_table, preferred_element_type=jnp.float32)
    spectrum = spectrum.astype(jnp.bfloat16).reshape(P_SIZE, R, NF, 2)
    sample_index = jnp.arange(NT, dtype=jnp.int32)

    def forward_one(index):
        kernel_real_part = kernel[0, index].astype(jnp.float32)
        kernel_imaginary = kernel[1, index].astype(jnp.float32)
        spectral_real = spectrum[:, :, index, 0].astype(jnp.float32)
        spectral_imaginary = spectrum[:, :, index, 1].astype(jnp.float32)
        wave_real = jnp.dot(spectral_real, kernel_real_part.T, precision=highest) - jnp.dot(spectral_imaginary, kernel_imaginary.T, precision=highest)
        wave_imag = jnp.dot(spectral_imaginary, kernel_real_part.T, precision=highest) + jnp.dot(spectral_real, kernel_imaginary.T, precision=highest)
        return jnp.stack([wave_real, wave_imag]).astype(jnp.bfloat16)

    waves = lax.map(forward_one, jnp.arange(NF, dtype=jnp.int32))

    def time_one(point):
        block = waves[:, :, point, :].reshape(2 * NF, S)
        signal = jnp.dot(block.T, inverse_table, preferred_element_type=jnp.float32)
        kept = jnp.where(sample_index[None, :] < onset_up[point][:, None], signal, 0.0).astype(jnp.bfloat16)
        back = jnp.dot(kept, forward_table, preferred_element_type=jnp.float32).astype(jnp.bfloat16)
        return kept, back

    upgoing, back_spectrum = lax.map(time_one, jnp.arange(P_SIZE, dtype=jnp.int32))
    back_spectrum = back_spectrum.reshape(P_SIZE, S, NF, 2)

    def adjoint_one(index):
        blocks = S // N_SRC
        backward_real = back_spectrum[:, :, index, 0].astype(jnp.float32).reshape(P_SIZE, N_SRC, blocks)
        backward_imaginary = back_spectrum[:, :, index, 1].astype(jnp.float32).reshape(P_SIZE, N_SRC, blocks)
        kernel_real_part = kernel[0, index].astype(jnp.float32).reshape(N_SRC, blocks, R)
        kernel_imaginary = kernel[1, index].astype(jnp.float32).reshape(N_SRC, blocks, R)
        term_real = jnp.einsum("pbs,bsr->bpr", backward_real, kernel_real_part, precision=highest) + jnp.einsum("pbs,bsr->bpr", backward_imaginary, kernel_imaginary, precision=highest)
        term_imag = jnp.einsum("pbs,bsr->bpr", backward_imaginary, kernel_real_part, precision=highest) - jnp.einsum("pbs,bsr->bpr", backward_real, kernel_imaginary, precision=highest)
        sum_real = lax.optimization_barrier(term_real.astype(jnp.bfloat16)).astype(jnp.float32).sum(0)
        sum_imag = lax.optimization_barrier(term_imag.astype(jnp.bfloat16)).astype(jnp.float32).sum(0)
        return jnp.stack([sum_real, sum_imag]).astype(jnp.bfloat16)

    adjoint = lax.map(adjoint_one, jnp.arange(NF, dtype=jnp.int32))

    def trace_one(point):
        block = adjoint[:, :, point, :].reshape(2 * NF, R)
        trace = jnp.dot(block.T, inverse_table, preferred_element_type=jnp.float32)
        cut = jnp.where(sample_index[None, :] < onset_back[point][:, None], trace, 0.0)
        return (direct[point].astype(jnp.float32) - cut).astype(jnp.bfloat16)

    updated = lax.map(trace_one, jnp.arange(P_SIZE, dtype=jnp.int32))
    return upgoing, updated
```

```python
import math

import jax
import jax.numpy as jnp
import ml_dtypes
import numpy as np
from jax import lax
from jax.experimental import pallas as pl
from jax.experimental.pallas import tpu as pltpu
from jax.sharding import PartitionSpec as P

BIN0 = 16


def band_tables(nt, nf):
    phase = np.arange(nt)[:, None] * (BIN0 + np.arange(nf))[None, :] % nt
    angle = phase.astype(np.float32) * np.float32(2.0 * math.pi / nt)
    both = np.stack([np.cos(angle), -np.sin(angle)], axis=2).reshape(nt, 2 * nf)
    both = both.astype(np.float32).T
    forward = both.astype(ml_dtypes.bfloat16)
    inverse = (np.float32(2.0 / nt) * both).astype(ml_dtypes.bfloat16)
    return np.ascontiguousarray(forward), np.ascontiguousarray(inverse)


NN = (((1,), (0,)), ((), ()))
NT_ = (((1,), (1,)), ((), ()))


def waves_kernel(pz, pf, spec_ref, kernel_ref, out_ref):
    nz, nf = spec_ref.shape[0], spec_ref.shape[1]
    x = jnp.concatenate(
        [
            jnp.concatenate([spec_ref[z, f, 0] for f in range(nf)], axis=1)
            for z in range(nz)
        ],
        axis=0,
    )
    a = lax.dot_general(x, kernel_ref[0, 0], NT_, preferred_element_type=jnp.float32)
    b = lax.dot_general(x, kernel_ref[1, 0], NT_, preferred_element_type=jnp.float32)
    for z in range(nz):
        r0, r1, r2 = 2 * z * pz, 2 * z * pz + pz, 2 * z * pz + 2 * pz
        real = a[r0:r1] - b[r1:r2]
        imag = a[r1:r2] + b[r0:r1]
        for h in range(pz // pf):
            rows = jnp.concatenate([real[h * pf : (h + 1) * pf], imag[h * pf : (h + 1) * pf]], axis=0)
            out_ref[z * (pz // pf) + h, 0] = rows.astype(jnp.bfloat16)


def terms_kernel(pz, pf, back_ref, kernel_ref, out_ref):
    nf = back_ref.shape[0]
    nz, rl = out_ref.shape[0], out_ref.shape[4]
    each = [back_ref[f, 0].astype(jnp.float32) for f in range(nf)]
    x = jnp.concatenate(
        [e[:pf] for e in each] + [e[pf:] for e in each], axis=0
    ).astype(jnp.bfloat16)
    half = nf * pf
    a = lax.dot_general(x, kernel_ref[0, 0], NN, preferred_element_type=jnp.float32)
    b = lax.dot_general(x, kernel_ref[1, 0], NN, preferred_element_type=jnp.float32)
    real = a[:half] + b[half:]
    imag = a[half:] - b[:half]
    for z in range(nz):
        rows = jnp.concatenate([real[z * pz : (z + 1) * pz], imag[z * pz : (z + 1) * pz]], axis=0)
        rows = rows.astype(jnp.bfloat16)
        for f in range(nf):
            out_ref[z, f, 0] = rows[:, f * rl : (f + 1) * rl]


def local(nf, nz, focusing, direct, kernel, onset_up, onset_back):
    pz, rl, nt = focusing.shape
    _, bins, sl, receivers = kernel.shape
    pf = onset_up.shape[0]
    forward, inverse = band_tables(nt, nf * bins)
    forward, inverse = jnp.asarray(forward), jnp.asarray(inverse)
    sample_index = jnp.arange(nt, dtype=jnp.int32)
    k_spec = pl.BlockSpec((2, 1, sl, receivers), lambda j: (0, j, 0, 0))
    params = pltpu.CompilerParams(vmem_limit_bytes=32 << 20)
    cost = pl.CostEstimate(
        flops=8 * bins * sl * receivers * nf * pf,
        bytes_accessed=4 * bins * sl * receivers,
        transcendentals=0,
    )

    spectrum = jnp.einsum("kt,prt->kpr", forward, focusing, preferred_element_type=jnp.float32)
    spectrum = spectrum.astype(jnp.bfloat16).reshape(nf, bins, 2 * pz, rl)
    grouped = lax.all_to_all(spectrum, "freq", split_axis=0, concat_axis=0, tiled=True)
    gathered = lax.all_gather(grouped, "src", axis=0, tiled=False)
    waves = pl.pallas_call(
        lambda *refs: waves_kernel(pz, pf, *refs),
        out_shape=jax.ShapeDtypeStruct((nf, bins, 2 * pf, sl), jnp.bfloat16),
        grid=(bins,),
        in_specs=[pl.BlockSpec((nz, nf, 1, 2 * pz, rl), lambda j: (0, 0, j, 0, 0)), k_spec],
        out_specs=pl.BlockSpec((nf, 1, 2 * pf, sl), lambda j: (0, j, 0, 0)),
        compiler_params=params,
        cost_estimate=cost,
        name="waves",
    )(gathered, kernel)
    timed = lax.all_to_all(waves, "freq", split_axis=0, concat_axis=0, tiled=True)
    signal = jnp.einsum(
        "kps,kt->pst",
        timed.reshape(2 * nf * bins, pf, sl),
        inverse,
        preferred_element_type=jnp.float32,
    )
    upgoing = jnp.where(sample_index[None, None, :] < onset_up[:, :, None], signal, 0.0).astype(
        jnp.bfloat16
    )
    back = jnp.einsum("kt,pst->kps", forward, upgoing, preferred_element_type=jnp.float32)
    back = back.astype(jnp.bfloat16).reshape(nf, bins, 2 * pf, sl)
    banded = lax.all_to_all(back, "freq", split_axis=0, concat_axis=0, tiled=True)
    terms = pl.pallas_call(
        lambda *refs: terms_kernel(pz, pf, *refs),
        out_shape=jax.ShapeDtypeStruct((nz, nf, bins, 2 * pz, rl), jnp.bfloat16),
        grid=(bins,),
        in_specs=[pl.BlockSpec((nf, 1, 2 * pf, sl), lambda j: (0, j, 0, 0)), k_spec],
        out_specs=pl.BlockSpec((nz, nf, 1, 2 * pz, rl), lambda j: (0, 0, j, 0, 0)),
        compiler_params=params,
        cost_estimate=cost,
        name="terms",
    )(banded, kernel)
    summed = lax.psum_scatter(terms, "src", scatter_dimension=0, tiled=False)
    spread = lax.all_to_all(summed, "freq", split_axis=0, concat_axis=0, tiled=True)
    trace = jnp.einsum(
        "kpr,kt->prt",
        spread.reshape(2 * nf * bins, pz, rl),
        inverse,
        preferred_element_type=jnp.float32,
    )
    cut = jnp.where(sample_index[None, None, :] < onset_back[:, :, None], trace, 0.0)
    updated = (direct.astype(jnp.float32) - cut).astype(jnp.bfloat16)
    return (upgoing, updated)


def solution(mesh):
    placed = (
        P("src", "freq", None),
        P("src", "freq", None),
        P(None, "freq", "src", None),
        P("freq", "src"),
        P("src", "freq"),
    )
    nf, nz = mesh.shape["freq"], mesh.shape["src"]
    return jax.shard_map(
        lambda *args: local(nf, nz, *args),
        mesh=mesh,
        in_specs=placed,
        out_specs=(P("freq", "src", None), P("src", "freq", None)),
        check_vma=False,
    )
```

```python
import math

import jax
import jax.numpy as jnp
import ml_dtypes
import numpy as np
from jax import lax
from jax.experimental import pallas as pl
from jax.experimental.pallas import tpu as pltpu
from jax.sharding import PartitionSpec as P

BIN0 = 16


def band_tables(nt, nf):
    phase = np.arange(nt)[:, None] * (BIN0 + np.arange(nf))[None, :] % nt
    angle = phase.astype(np.float32) * np.float32(2.0 * math.pi / nt)
    both = np.stack([np.cos(angle), -np.sin(angle)], axis=2).reshape(nt, 2 * nf)
    both = both.astype(np.float32).T
    forward = both.astype(ml_dtypes.bfloat16)
    inverse = (np.float32(2.0 / nt) * both).astype(ml_dtypes.bfloat16)
    return np.ascontiguousarray(forward), np.ascontiguousarray(inverse)


NN = (((1,), (0,)), ((), ()))
NT_ = (((1,), (1,)), ((), ()))


MESH = pl.DeviceIdType.MESH
LAG = 2
SLOTS = 3


def chunk_bins(bins):
    return 2 if bins % 2 == 0 else 1


def enter(f, z, nf, nz):
    barrier = pltpu.get_barrier_semaphore()
    for step in range(1, nf):
        pl.semaphore_signal(barrier, inc=1, device_id={"freq": lax.rem(f + step, nf)}, device_id_type=MESH)

    @pl.when(z > 0)
    def _():
        pl.semaphore_signal(barrier, inc=1, device_id={"src": z - 1}, device_id_type=MESH)

    @pl.when(z < nz - 1)
    def _():
        pl.semaphore_signal(barrier, inc=1, device_id={"src": z + 1}, device_id_type=MESH)

    near = jnp.where(z > 0, 1, 0) + jnp.where(z < nz - 1, 1, 0)
    pl.semaphore_wait(barrier, nf - 1 + near)


def remote(src, dst, send, recv, axis, index):
    return pltpu.make_async_remote_copy(
        src_ref=src, dst_ref=dst, send_sem=send, recv_sem=recv, device_id={axis: index}, device_id_type=MESH
    )


def settle(ref, sem):
    pltpu.make_async_copy(ref, ref, sem).wait()


def fetch(kern, kbuf, ksem, j):
    slot = lax.rem(j, SLOTS)
    return pltpu.make_async_copy(kern.at[:, j], kbuf.at[slot], ksem.at[slot])


def waves_kernel(
    nf, nz, pz, pf, spec, kern, out, gat, own, kbuf, ksem, lsem, osem, a_send, a_recv, z_send, z_recv, w_send, w_recv
):
    f, z = lax.axis_index("freq"), lax.axis_index("src")
    bins = spec.shape[1]
    chunk = chunk_bins(bins)
    count = bins // chunk

    def part(c):
        return pl.ds(c * chunk, chunk)

    for j in range(SLOTS):
        fetch(kern, kbuf, ksem, j).start()
    mine = pltpu.make_async_copy(spec.at[f], gat.at[z, f], lsem)
    mine.start()
    enter(f, z, nf, nz)

    def scatter(c, carry):
        for step in range(1, nf):
            t = lax.rem(f + step, nf)
            remote(
                spec.at[t, part(c)], gat.at[z, f, part(c)], a_send.at[step], a_recv.at[c], "freq", t
            ).start()
        return carry

    lax.fori_loop(0, count, scatter, 0)
    mine.wait()

    def pass_on(s, c, right):
        to = z + 1 if right else z - 1
        fits = z < nz - 1 if right else z > 0

        @pl.when(fits)
        def _():
            block = gat.at[s, :, part(c)]
            remote(block, block, z_send.at[0 if right else 1, s], z_recv.at[s, c], "src", to).start()

    def multiply(j):
        fetch(kern, kbuf, ksem, j).wait()
        slot = lax.rem(j, SLOTS)
        x = jnp.concatenate(
            [jnp.concatenate([gat[s, r, j] for r in range(nf)], axis=1) for s in range(nz)], axis=0
        )
        a = lax.dot_general(x, kbuf[slot, 0], NT_, preferred_element_type=jnp.float32)
        b = lax.dot_general(x, kbuf[slot, 1], NT_, preferred_element_type=jnp.float32)
        for s in range(nz):
            r0, r1, r2 = 2 * s * pz, 2 * s * pz + pz, 2 * s * pz + 2 * pz
            real = a[r0:r1] - b[r1:r2]
            imag = a[r1:r2] + b[r0:r1]
            for h in range(pz // pf):
                rows = jnp.concatenate([real[h * pf : (h + 1) * pf], imag[h * pf : (h + 1) * pf]], axis=0)
                own[s * (pz // pf) + h, j] = rows.astype(jnp.bfloat16)

        @pl.when(j + SLOTS < bins)
        def _():
            fetch(kern, kbuf, ksem, j + SLOTS).start()

    def iteration(i, carry):
        @pl.when(i < count)
        def _():
            settle(gat.at[z, pl.ds(0, nf - 1), part(i)], a_recv.at[i])
            pass_on(z, i, True)
            pass_on(z, i, False)

        for d in range(1, nz):
            c = i - LAG * d

            @pl.when((c >= 0) & (c < count) & (z - d >= 0))
            def _():
                settle(gat.at[z - d, :, part(c)], z_recv.at[z - d, c])
                pass_on(z - d, c, True)

            @pl.when((c >= 0) & (c < count) & (z + d < nz))
            def _():
                settle(gat.at[z + d, :, part(c)], z_recv.at[z + d, c])
                pass_on(z + d, c, False)

        c = i - LAG * (nz - 1)

        @pl.when((c >= 0) & (c < count))
        def _():
            for k in range(chunk):
                multiply(c * chunk + k)
            pltpu.make_async_copy(own.at[f, part(c)], out.at[f, part(c)], osem).start()
            for step in range(1, nf):
                t = lax.rem(f + step, nf)
                remote(
                    own.at[t, part(c)], out.at[f, part(c)], w_send.at[step], w_recv.at[step], "freq", t
                ).start()

        return carry

    lax.fori_loop(0, count + LAG * (nz - 1), iteration, 0)
    settle(out.at[f], osem)
    for step in range(1, nf):
        settle(out.at[lax.rem(f + nf - step, nf)], w_recv.at[step])
        settle(own.at[lax.rem(f + step, nf)], w_send.at[step])
        settle(spec.at[lax.rem(f + step, nf)], a_send.at[step])
    for s in range(nz):

        @pl.when((s <= z) & (z < nz - 1))
        def _():
            settle(gat.at[s], z_send.at[0, s])

        @pl.when((s >= z) & (z > 0))
        def _():
            settle(gat.at[s], z_send.at[1, s])


def terms_kernel(
    nf, nz, pz, pf, back, kern, out, held, term, left, right, total, kbuf, ksem, lsem, osem,
    h_send, h_recv, z_send, z_recv, w_send, w_recv
):
    f, z = lax.axis_index("freq"), lax.axis_index("src")
    bins = back.shape[1]
    rl = out.shape[3]
    chunk = chunk_bins(bins)
    count = bins // chunk
    half = nf * pf

    def part(c):
        return pl.ds(c * chunk, chunk)

    for j in range(SLOTS):
        fetch(kern, kbuf, ksem, j).start()
    mine = pltpu.make_async_copy(back.at[f], held.at[f], lsem)
    mine.start()

    @pl.when(z == 0)
    def _():
        left[0] = jnp.zeros(left.shape[1:], left.dtype)

    @pl.when(z == nz - 1)
    def _():
        right[nz - 1] = jnp.zeros(right.shape[1:], right.dtype)

    enter(f, z, nf, nz)

    def scatter(c, carry):
        for step in range(1, nf):
            t = lax.rem(f + step, nf)
            remote(
                back.at[t, part(c)], held.at[f, part(c)], h_send.at[step], h_recv.at[c], "freq", t
            ).start()
        return carry

    lax.fori_loop(0, count, scatter, 0)
    mine.wait()

    def multiply(j):
        fetch(kern, kbuf, ksem, j).wait()
        slot = lax.rem(j, SLOTS)
        each = [held[r, j].astype(jnp.float32) for r in range(nf)]
        x = jnp.concatenate([e[:pf] for e in each] + [e[pf:] for e in each], axis=0).astype(jnp.bfloat16)
        a = lax.dot_general(x, kbuf[slot, 0], NN, preferred_element_type=jnp.float32)
        b = lax.dot_general(x, kbuf[slot, 1], NN, preferred_element_type=jnp.float32)
        real = a[:half] + b[half:]
        imag = a[half:] - b[:half]
        for s in range(nz):
            rows = jnp.concatenate([real[s * pz : (s + 1) * pz], imag[s * pz : (s + 1) * pz]], axis=0)
            rows = rows.astype(jnp.bfloat16)
            for r in range(nf):
                term[s, j, r] = rows[:, r * rl : (r + 1) * rl]

        @pl.when(j + SLOTS < bins)
        def _():
            fetch(kern, kbuf, ksem, j + SLOTS).start()

    def add(d, c, held_sum):
        summed = term[d, part(c)].astype(jnp.float32) + held_sum[d, part(c)].astype(jnp.float32)
        term[d, part(c)] = summed.astype(jnp.bfloat16)

    def iteration(i, carry):
        @pl.when(i < count)
        def _():
            settle(held.at[pl.ds(0, nf - 1), part(i)], h_recv.at[i])
            for k in range(chunk):
                multiply(i * chunk + k)

        c0 = i - LAG * z
        c1 = i - LAG * (nz - 1 - z)
        for d in range(nz - 1, 0, -1):

            @pl.when((c0 >= 0) & (c0 < count) & (z < d))
            def _():
                @pl.when(z > 0)
                def _():
                    settle(left.at[d, part(c0)], z_recv.at[0, d, c0])
                    add(d, c0, left)

                remote(
                    term.at[d, part(c0)], left.at[d, part(c0)], z_send.at[d], z_recv.at[0, d, c0], "src", z + 1
                ).start()

        for d in range(nz - 1):

            @pl.when((c1 >= 0) & (c1 < count) & (z > d))
            def _():
                @pl.when(z < nz - 1)
                def _():
                    settle(right.at[d, part(c1)], z_recv.at[1, d, c1])
                    add(d, c1, right)

                remote(
                    term.at[d, part(c1)], right.at[d, part(c1)], z_send.at[d], z_recv.at[1, d, c1], "src", z - 1
                ).start()

        c = i - LAG * jnp.maximum(z, nz - 1 - z)

        @pl.when((c >= 0) & (c < count))
        def _():
            @pl.when(z > 0)
            def _():
                settle(left.at[z, part(c)], z_recv.at[0, z, c])

            @pl.when(z < nz - 1)
            def _():
                settle(right.at[z, part(c)], z_recv.at[1, z, c])

            summed = (
                term[z, part(c)].astype(jnp.float32)
                + left[z, part(c)].astype(jnp.float32)
                + right[z, part(c)].astype(jnp.float32)
            ).astype(jnp.bfloat16)
            for r in range(nf):
                total[r, part(c)] = summed[:, r]
            pltpu.make_async_copy(total.at[f, part(c)], out.at[f, part(c)], osem).start()
            for step in range(1, nf):
                t = lax.rem(f + step, nf)
                remote(
                    total.at[t, part(c)], out.at[f, part(c)], w_send.at[step], w_recv.at[step], "freq", t
                ).start()

        return carry

    lax.fori_loop(0, count + LAG * (nz - 1), iteration, 0)
    settle(out.at[f], osem)
    for step in range(1, nf):
        settle(out.at[lax.rem(f + nf - step, nf)], w_recv.at[step])
        settle(total.at[lax.rem(f + step, nf)], w_send.at[step])
        settle(back.at[lax.rem(f + step, nf)], h_send.at[step])
    for d in range(nz):

        @pl.when(d != z)
        def _():
            settle(term.at[d], z_send.at[d])


def local(nf, nz, focusing, direct, kernel, onset_up, onset_back):
    pz, rl, nt = focusing.shape
    _, bins, sl, receivers = kernel.shape
    pf = onset_up.shape[0]
    forward, inverse = band_tables(nt, nf * bins)
    forward, inverse = jnp.asarray(forward), jnp.asarray(inverse)
    sample_index = jnp.arange(nt, dtype=jnp.int32)
    count = bins // chunk_bins(bins)
    anywhere = pl.BlockSpec(memory_space=pl.ANY)
    dma = pltpu.SemaphoreType.DMA
    vmem = lambda *shape: pltpu.VMEM(shape, jnp.bfloat16)
    params = lambda n: pltpu.CompilerParams(vmem_limit_bytes=40 << 20, collective_id=n, has_side_effects=True)
    common = [vmem(SLOTS, 2, sl, receivers), dma((SLOTS,)), dma, dma, dma((nf,)), dma((count,))]
    cost = pl.CostEstimate(
        flops=8 * bins * sl * receivers * nf * pf,
        bytes_accessed=4 * bins * sl * receivers,
        transcendentals=0,
    )

    spectrum = jnp.einsum("kt,prt->kpr", forward, focusing, preferred_element_type=jnp.float32)
    spectrum = spectrum.astype(jnp.bfloat16).reshape(nf, bins, 2 * pz, rl)
    timed = pl.pallas_call(
        lambda *refs: waves_kernel(nf, nz, pz, pf, *refs),
        out_shape=jax.ShapeDtypeStruct((nf, bins, 2 * pf, sl), jnp.bfloat16),
        in_specs=[anywhere, anywhere],
        out_specs=anywhere,
        scratch_shapes=[vmem(nz, nf, bins, 2 * pz, rl), vmem(nf, bins, 2 * pf, sl)]
        + common
        + [dma((2, nz)), dma((nz, count)), dma((nf,)), dma((nf,))],
        compiler_params=params(0),
        cost_estimate=cost,
        name="waves",
    )(spectrum, kernel)
    signal = jnp.einsum(
        "kps,kt->pst",
        timed.reshape(2 * nf * bins, pf, sl),
        inverse,
        preferred_element_type=jnp.float32,
    )
    upgoing = jnp.where(sample_index[None, None, :] < onset_up[:, :, None], signal, 0.0).astype(
        jnp.bfloat16
    )
    back = jnp.einsum("kt,pst->kps", forward, upgoing, preferred_element_type=jnp.float32)
    back = back.astype(jnp.bfloat16).reshape(nf, bins, 2 * pf, sl)
    spread = pl.pallas_call(
        lambda *refs: terms_kernel(nf, nz, pz, pf, *refs),
        out_shape=jax.ShapeDtypeStruct((nf, bins, 2 * pz, rl), jnp.bfloat16),
        in_specs=[anywhere, anywhere],
        out_specs=anywhere,
        scratch_shapes=[vmem(nf, bins, 2 * pf, sl)]
        + [vmem(nz, bins, nf, 2 * pz, rl)] * 3
        + [vmem(nf, bins, 2 * pz, rl)]
        + common
        + [dma((nz,)), dma((2, nz, count)), dma((nf,)), dma((nf,))],
        compiler_params=params(1),
        cost_estimate=cost,
        name="terms",
    )(back, kernel)
    trace = jnp.einsum(
        "kpr,kt->prt",
        spread.reshape(2 * nf * bins, pz, rl),
        inverse,
        preferred_element_type=jnp.float32,
    )
    cut = jnp.where(sample_index[None, None, :] < onset_back[:, :, None], trace, 0.0)
    updated = (direct.astype(jnp.float32) - cut).astype(jnp.bfloat16)
    return (upgoing, updated)


def solution(mesh):
    placed = (
        P("src", "freq", None),
        P("src", "freq", None),
        P(None, "freq", "src", None),
        P("freq", "src"),
        P("src", "freq"),
    )
    nf, nz = mesh.shape["freq"], mesh.shape["src"]
    return jax.shard_map(
        lambda *args: local(nf, nz, *args),
        mesh=mesh,
        in_specs=placed,
        out_specs=(P("freq", "src", None), P("src", "freq", None)),
        check_vma=False,
    )
```
